32 devices in a mesh: dp: 16 (over z, y, x), owner: 2 (over core).
Axes of the slice: x: 2, y: 2, z: 4, core: 2. Of those that a mesh axis runs over, the one named last changes fastest.
Arguments:
- query_out: bfloat16 [128, 4096], P('dp', 'owner'), may hold values from -6 to 6
- query_in: bfloat16 [128, 8192], P('dp'), may hold values from -6 to 6
- train_out: bfloat16 [128, 4096], P('dp', 'owner'), may hold values from -6 to 6
- train_in: bfloat16 [128, 8192], P('dp'), may hold values from -6 to 6
- basis_out: bfloat16 [24, 256, 256], P('owner'), may hold values from -1 to 1, as said below
- basis_in: bfloat16 [64, 128, 128], P('dp'), may hold values from -1 to 1, as said below
- eigvals: float32 [6144, 8192], P('owner', 'dp'), may hold values from 0.1 to 10
- owner_map: int32 [16], replicated, may hold values from 0 to 1, as said below
Outputs:
- scores: float32 [8, 8], replicated
The draws below stay inside these ranges and needn't reach their ends.
Inputs may be any that keep to these rules, and one draw needn't show every extreme that they name: owner_map[b] is the owner of hidden block b. Blocks form ranges of 8 in order; a block of range r is owned by r or by r xor 1. Of two such partner owners one holds exactly 12 blocks and keeps 12 // 2 of its own range, the other holds 4 blocks and keeps 8 - 12 // 2 of its own range. `basis_out`: each [256, 256] block is an orthogonal matrix rounded to bfloat16; block o * 12 + s belongs to the s-th block, in block order, that owner o holds; blocks past an owner's count are not read. `basis_in`: each [128, 128] block is an orthogonal matrix rounded to bfloat16.
All inputs are finite; a program needn't handle non-finite values.
Results may differ from the reference program's by a relative error of at most 0.0067.
Values may be sent and summed in bfloat16 or wider, within the bound.
A program may use at most 128 MiB of HBM per device.

```python
import math
import jax
import jax.numpy as jnp
from jax import lax

D = 8192
BK = 256
BA = 128
BLK_OWN = 8
CAP = 12
NQ = 8
ET = 16
F = 4096
NB = 16
QTOK = 128
QT = 16
TT = 128
NE = 8
N_OWNER = 2


def orthogonal_blocks(key, block_count, block_size):
    normal = jax.random.normal(key, (block_count, block_size, block_size), jnp.float32)
    basis_q, upper_part = jnp.linalg.qr(normal)
    sign_fix = jnp.sign(jnp.diagonal(upper_part, axis1=1, axis2=2))
    sign_fix = jnp.where(sign_fix == 0, 1.0, sign_fix)
    return basis_q * sign_fix[:, None, :]


def draw_basis_out(key, part):
    return orthogonal_blocks(jax.random.fold_in(key, 11), N_OWNER * CAP, BK).astype(jnp.bfloat16)


def draw_basis_in(key, part):
    return orthogonal_blocks(jax.random.fold_in(key, 13), D // BA, BA).astype(jnp.bfloat16)


def draw_owner_map(key, part):
    pair_total = N_OWNER // 2
    heavy_bits = jax.random.randint(jax.random.fold_in(key, 21), (pair_total,), 0, 2).astype(jnp.int32)
    range_ids = jnp.arange(N_OWNER, dtype=jnp.int32)
    shuffled = jax.vmap(lambda range_index: jax.random.permutation(jax.random.fold_in(key, 1000 + range_index), BLK_OWN))(range_ids)
    position = jnp.argsort(shuffled, axis=1).astype(jnp.int32)
    heavy = range_ids // 2 * 2 + heavy_bits[range_ids // 2]
    keep_count = jnp.where(range_ids == heavy, CAP // 2, BLK_OWN - CAP // 2)
    partner = jnp.bitwise_xor(range_ids, 1)
    owners = jnp.where(position < keep_count[:, None], range_ids[:, None], partner[:, None])
    return owners.reshape(N_OWNER * BLK_OWN).astype(jnp.int32)


def block_levels(stream_key, shape, cuts, low, high):
    loudness, own = 1.0, jax.random.fold_in(stream_key, 6)
    for dim, shards_of in cuts:
        draws = jnp.exp(jax.random.uniform(jax.random.fold_in(own, dim), (shards_of,), jnp.float32, low / len(cuts), high / len(cuts)))
        loudness = loudness * jnp.repeat(draws, shape[dim] // shards_of).reshape([-1 if axis == dim else 1 for axis in range(len(shape))])
    return loudness


def normal_values(stream_key, extent, spread, bound, shards=(), held_as=jnp.bfloat16):
    loudness = block_levels(stream_key, extent, shards, -0.22, 0.18) if shards else 1.0
    array = jax.random.normal(stream_key, extent, jnp.float32) * spread * loudness
    return jnp.minimum(jnp.maximum(array, -bound), bound).astype(held_as)


def setup_inputs(seed: int = 0) -> dict:
    keys = jax.random.split(jax.random.key(seed), 9)
    query_out = normal_values(keys[0], (QTOK, F), 1.0, 6.0, ((0, 16), (1, 2)))
    query_in = normal_values(keys[1], (QTOK, D), 1.0, 6.0, ((0, 16),))
    train_out = normal_values(keys[2], (TT, F), 1.0, 6.0, ((0, 16), (1, 2)))
    train_in = normal_values(keys[3], (TT, D), 1.0, 6.0, ((0, 16),))
    basis_out = draw_basis_out(jax.random.fold_in(keys[8], 71), 0)
    basis_in = draw_basis_in(jax.random.fold_in(keys[8], 71), 0)
    eigvals = jnp.clip(jnp.exp(math.log(10.0) - 4.6051702 * jax.random.uniform(keys[6], (N_OWNER * CAP * BK, D), jnp.float32) ** block_levels(keys[6], (N_OWNER * CAP * BK, D), ((0, 2), (1, 16)), -0.2, 0.2)), 0.1, 10.0)
    owner_map = draw_owner_map(jax.random.fold_in(keys[8], 71), 0)
    return {"query_out": query_out, "query_in": query_in, "train_out": train_out, "train_in": train_in, "basis_out": basis_out, "basis_in": basis_in, "eigvals": eigvals, "owner_map": owner_map}


DAMPING = 0.1

def rotate_columns(values, basis_in):
    token_count = values.shape[0]
    blocks = values.reshape(token_count, D // BA, BA).astype(jnp.float32)
    turned = jnp.einsum('tnb,nbc->tnc', blocks, basis_in.astype(jnp.float32))
    return turned.astype(jnp.bfloat16).reshape(token_count, D)

def reference(query_out, query_in, train_out, train_in, basis_out, basis_in, eigvals, owner_map):
    block_ids = jnp.arange(NB, dtype=jnp.int32)
    same_owner = owner_map[None, :] == owner_map[:, None]
    earlier = block_ids[None, :] < block_ids[:, None]
    slot_rank = lax.optimization_barrier(jnp.sum((same_owner & earlier).astype(jnp.int32), axis=1)).astype(jnp.int32)
    slot_index = (owner_map * CAP + slot_rank).astype(jnp.int32)
    query_act = rotate_columns(query_in, basis_in)
    train_inputs = train_in.reshape(NE, ET, D).astype(jnp.float32)
    basis_in_wide = basis_in.astype(jnp.float32)

    def one_block(block_index):
        slot_now = slot_index[block_index]
        eig_basis = lax.dynamic_index_in_dim(basis_out, slot_now, 0, keepdims=False)
        first_unit = (block_index * BK).astype(jnp.int32)
        query_block = lax.dynamic_slice_in_dim(query_out, first_unit, BK, 1)
        query_rot = jnp.dot(query_block.astype(jnp.float32), eig_basis.astype(jnp.float32), preferred_element_type=jnp.float32).astype(jnp.bfloat16)
        shifted = lax.dynamic_slice_in_dim(eigvals, (slot_now * BK).astype(jnp.int32), BK, 0) + DAMPING
        train_block = lax.dynamic_slice_in_dim(train_out, first_unit, BK, 1).reshape(NE, ET, BK).astype(jnp.float32)
        example_grad = jnp.einsum('etk,etd->ekd', train_block, train_inputs)

        def one_query(query_index):
            first_row = (query_index * QT).astype(jnp.int32)
            left_side = lax.dynamic_slice_in_dim(query_rot, first_row, QT, 0)
            right_side = lax.dynamic_slice_in_dim(query_act, first_row, QT, 0)
            moment = jnp.dot(left_side.T.astype(jnp.float32), right_side.astype(jnp.float32), preferred_element_type=jnp.float32)
            damped = (moment / shifted).astype(jnp.bfloat16)
            half_back = jnp.einsum('knb,ncb->knc', damped.reshape(BK, D // BA, BA).astype(jnp.float32), basis_in_wide)
            half_back = half_back.astype(jnp.bfloat16).reshape(BK, D)
            precond = jnp.dot(eig_basis.astype(jnp.float32), half_back.astype(jnp.float32), preferred_element_type=jnp.float32).astype(jnp.bfloat16)
            return jnp.einsum('kd,ekd->e', precond.astype(jnp.float32), example_grad)
        return lax.map(one_query, jnp.arange(NQ, dtype=jnp.int32))
    totals = lax.map(one_block, block_ids)
    score_scale = 1.0 / math.sqrt(QT * ET * F * D)
    return lax.optimization_barrier(jnp.sum(totals, axis=0)) * score_scale
```

```python
import functools
import math

import jax
import jax.numpy as jnp
from jax import lax
from jax.experimental import pallas as pl
from jax.experimental.pallas import tpu as pltpu
from jax.sharding import PartitionSpec as P

NQ = 8
ET = 16
DAMPING = 0.1
MESH = pl.DeviceIdType.MESH
F32 = jnp.float32
BF16 = jnp.bfloat16


def flipped(index, mask, bits):
    for k in range(bits):
        if mask >> k & 1:
            index = index + (1 << k) - (2 << k) * (index // (1 << k) % 2)
    return index


def kernel(
    n, m, local_q, example_count, scale,
    map_ref, out_tok, in_tok, basis_out_hbm, basis_in_hbm, eig_hbm,
    scores_ref,
    gathered, cols, basis_out, basis_in, eig, masked, act_t, acc, parts, owner_parts,
    ag_send, ag_recv, core_send, core_recv, a2a_send, a2a_recv, load_sem,
    part_send, part_recv, own_send, own_recv,
):
    d = lax.axis_index("dp")
    o = lax.axis_index("owner")
    bits = n.bit_length() - 1
    partner = flipped(o, 1, 1)
    blocks = out_tok.shape[0]
    width = out_tok.shape[2]
    capacity = basis_out.shape[0]
    in_blocks, in_width = basis_in.shape[0], basis_in.shape[1]
    rows = n * out_tok.shape[1]
    per_device = out_tok.shape[1]
    half = blocks // 2
    own = o % 2 * blocks

    loads = [
        pltpu.make_async_copy(basis_in_hbm, basis_in, load_sem.at[0]),
        pltpu.make_async_copy(basis_out_hbm, basis_out, load_sem.at[1]),
        pltpu.make_async_copy(eig_hbm, eig, load_sem.at[2]),
    ]
    for load in loads:
        load.start()
    gathered[d, pl.ds(own, blocks)] = out_tok[...]
    cols[d] = in_tok[d]

    barrier = pltpu.get_barrier_semaphore()
    for r in range(1, n):
        pl.semaphore_signal(
            barrier, inc=1, device_id={"dp": (d + r) % n, "owner": o}, device_id_type=MESH
        )
    for r in range(1, m):
        pl.semaphore_signal(
            barrier, inc=1, device_id={"dp": d, "owner": (o + r) % m}, device_id_type=MESH
        )
    pl.semaphore_wait(barrier, n - 1 + m - 1)

    def piece(h, mask):
        return gathered.at[flipped(d, mask, bits), pl.ds(own + h * half, half)]

    def far_piece(h, mask):
        return gathered.at[
            flipped(d, mask, bits), pl.ds(blocks - own + h * half, half)
        ]

    def gather_copy(h, mask, k):
        return pltpu.make_async_remote_copy(
            src_ref=piece(h, mask),
            dst_ref=piece(h, mask),
            send_sem=ag_send.at[h, mask ^ (1 << k)],
            recv_sem=ag_recv.at[h, mask ^ (1 << k)],
            device_id={"dp": flipped(d, 1 << k, bits), "owner": o},
            device_id_type=MESH,
        )

    def gather_arrival(h, mask):
        return pltpu.make_async_remote_copy(
            src_ref=piece(h, mask),
            dst_ref=piece(h, mask),
            send_sem=ag_send.at[h, mask],
            recv_sem=ag_recv.at[h, mask],
            device_id={"dp": flipped(d, 1, bits), "owner": o},
            device_id_type=MESH,
        )

    def core_copy(h, mask, ref):
        return pltpu.make_async_remote_copy(
            src_ref=ref,
            dst_ref=ref,
            send_sem=core_send.at[h, mask],
            recv_sem=core_recv.at[h, mask],
            device_id={"dp": d, "owner": partner},
            device_id_type=MESH,
        )

    def column_copy(r):
        return pltpu.make_async_remote_copy(
            src_ref=in_tok.at[(d + r) % n],
            dst_ref=cols.at[d],
            send_sem=a2a_send.at[r],
            recv_sem=a2a_recv.at[r],
            device_id={"dp": (d + r) % n, "owner": o},
            device_id_type=MESH,
        )

    def column_arrival(r):
        source = (d + n - r) % n
        return pltpu.make_async_remote_copy(
            src_ref=in_tok.at[source],
            dst_ref=cols.at[source],
            send_sem=a2a_send.at[r],
            recv_sem=a2a_recv.at[r],
            device_id={"dp": source, "owner": o},
            device_id_type=MESH,
        )

    first = list(range(bits - 1, -1, -1))
    second = first[:-2] + first[-2:][::-1]
    orders = (first, second)
    known = [[0], [0]]
    sent = []

    def prepare():
        for r in range(1, n):
            column_arrival(r).wait_recv()
        loads[0].wait()
        row = lax.broadcasted_iota(jnp.int32, (rows, in_width), 0)
        inside = row % per_device
        token = row // per_device * local_q + inside
        per_query = n * local_q // NQ
        owner_query = jnp.where(inside < local_q, token // per_query, NQ)
        for j in range(in_blocks):
            at = slice(j * in_width, (j + 1) * in_width)
            columns = cols[:, :, at].reshape(rows, in_width)
            turned = jnp.dot(columns, basis_in[j], preferred_element_type=F32)
            act_t[at, :] = turned.T.astype(BF16)
            for q in range(NQ):
                masked[q, :, at] = jnp.where(owner_query == q, turned, 0.0).astype(BF16)

    for step in range(bits):
        for h in range(2):
            k = orders[h][step]
            for mask in known[h]:
                copy = gather_copy(h, mask, k)
                copy.start()
                sent.append(copy)
        if step == 0:
            for h in range(2):
                copy = core_copy(h, 0, piece(h, 0))
                copy.start()
                sent.append(copy)
            for r in range(1, n):
                copy = column_copy(r)
                copy.start()
                sent.append(copy)
        if step == bits - 1:
            prepare()
        for h in range(2):
            k = orders[h][step]
            fresh = [mask ^ (1 << k) for mask in known[h]]
            for mask in fresh:
                gather_arrival(h, mask).wait_recv()
                copy = core_copy(h, mask, piece(h, mask))
                copy.start()
                sent.append(copy)
            known[h] += fresh
    for h in range(2):
        for mask in range(n):
            core_copy(h, mask, far_piece(h, mask)).wait_recv()
    for load in loads[1:]:
        load.wait()

    acc[...] = jnp.zeros_like(acc)
    base = o // 2 * 2 * blocks
    ranks, held = [], []
    count = 0
    for c in range(2 * blocks):
        mine = (map_ref[base + c] == o).astype(jnp.int32)
        held.append(mine)
        ranks.append(count)
        count = count + mine

    def one_slot(s, carry):
        block = 0
        for c in range(2 * blocks):
            block = block + c * held[c] * (ranks[c] == s).astype(jnp.int32)
        tokens = gathered[:, block].reshape(rows, width)
        turned = jnp.dot(tokens, basis_out[s], preferred_element_type=F32)
        turned = jnp.where(s < count, turned, 0.0)
        turned_t = turned.T
        left = turned_t.astype(BF16)
        start = pl.multiple_of(s * width, width)
        weight = 1.0 / (eig[pl.ds(start, width), :] + DAMPING)
        for q in range(NQ):
            moment = jnp.dot(left, masked[q], preferred_element_type=F32)
            damped = (moment * weight).astype(BF16)
            projected = jnp.dot(damped, act_t[...], preferred_element_type=F32)
            acc[q] += jnp.sum((projected * turned_t).reshape(-1, 8, rows), axis=0)
        return carry

    lax.fori_loop(0, capacity, one_slot, 0)

    per_token = jnp.sum(acc[...], axis=1)
    row = lax.broadcasted_iota(jnp.int32, (rows, 128), 0)
    inside = row % per_device
    token = row // per_device * (per_device - local_q) + inside - local_q
    example = lax.broadcasted_iota(jnp.int32, (rows, 128), 1)
    hot = jnp.where((inside >= local_q) & (token // ET == example), 1.0, 0.0)
    mine = jnp.dot(
        per_token, hot, precision=lax.Precision.HIGHEST, preferred_element_type=F32
    )

    parts[d] = mine

    def part_copy(r, source):
        return pltpu.make_async_remote_copy(
            src_ref=parts.at[source],
            dst_ref=parts.at[source],
            send_sem=part_send.at[r],
            recv_sem=part_recv.at[r],
            device_id={"dp": (d + r) % n, "owner": o},
            device_id_type=MESH,
        )

    def owner_copy(r, source):
        return pltpu.make_async_remote_copy(
            src_ref=owner_parts.at[source],
            dst_ref=owner_parts.at[source],
            send_sem=own_send.at[r],
            recv_sem=own_recv.at[r],
            device_id={"dp": d, "owner": (o + r) % m},
            device_id_type=MESH,
        )

    for r in range(1, n):
        copy = part_copy(r, d)
        copy.start()
        sent.append(copy)
    for r in range(1, n):
        part_copy(r, (d + n - r) % n).wait_recv()
    owner_parts[o] = jnp.sum(parts[...], axis=0)
    for r in range(1, m):
        copy = owner_copy(r, o)
        copy.start()
        sent.append(copy)
    for r in range(1, m):
        owner_copy(r, (o + m - r) % m).wait_recv()
    total = jnp.sum(owner_parts[...], axis=0) * scale
    scores_ref[...] = total[:, :example_count]
    for copy in sent:
        copy.wait_send()


def local(query_out, query_in, train_out, train_in, basis_out, basis_in, eigvals, owner_map):
    n = lax.axis_size("dp")
    m = lax.axis_size("owner")
    capacity, width = basis_out.shape[0], basis_out.shape[1]
    local_q = query_out.shape[0]
    per_device = local_q + train_out.shape[0]
    blocks = query_out.shape[1] // width
    units = eigvals.shape[1]
    rows = n * per_device
    example_count = n * train_out.shape[0] // ET
    out_tok = (
        jnp.concatenate([query_out, train_out], 0)
        .reshape(per_device, blocks, width)
        .transpose(1, 0, 2)
    )
    in_tok = (
        jnp.concatenate([query_in, train_in], 0)
        .reshape(per_device, n, units)
        .transpose(1, 0, 2)
    )
    hidden_total = query_out.shape[1] * m
    per_query = n * local_q // NQ
    scale = 1.0 / math.sqrt(per_query * ET * hidden_total * query_in.shape[1])
    vmem = pl.BlockSpec(memory_space=pltpu.VMEM)
    anywhere = pl.BlockSpec(memory_space=pl.ANY)
    dma = pltpu.SemaphoreType.DMA
    return pl.pallas_call(
        functools.partial(kernel, n, m, local_q, example_count, scale),
        out_shape=jax.ShapeDtypeStruct((NQ, example_count), F32),
        in_specs=[
            pl.BlockSpec(memory_space=pltpu.SMEM),
            vmem,
            vmem,
            anywhere,
            anywhere,
            anywhere,
        ],
        out_specs=vmem,
        scratch_shapes=[
            pltpu.VMEM((n, 2 * blocks, per_device, width), BF16),
            pltpu.VMEM((n, per_device, units), BF16),
            pltpu.VMEM(basis_out.shape, BF16),
            pltpu.VMEM(basis_in.shape, BF16),
            pltpu.VMEM(eigvals.shape, F32),
            pltpu.VMEM((NQ, rows, units), BF16),
            pltpu.VMEM((units, rows), BF16),
            pltpu.VMEM((NQ, 8, rows), F32),
            pltpu.VMEM((n, NQ, 128), F32),
            pltpu.VMEM((m, NQ, 128), F32),
            dma((2, n)),
            dma((2, n)),
            dma((2, n)),
            dma((2, n)),
            dma((n,)),
            dma((n,)),
            dma((3,)),
            dma((n,)),
            dma((n,)),
            dma((m,)),
            dma((m,)),
        ],
        compiler_params=pltpu.CompilerParams(
            collective_id=0, has_side_effects=True, vmem_limit_bytes=56 * 2**20
        ),
    )(owner_map, out_tok, in_tok, basis_out, basis_in, eigvals)


def solution(mesh):
    in_specs = (
        P("dp", "owner"),
        P("dp", None),
        P("dp", "owner"),
        P("dp", None),
        P("owner", None, None),
        P("dp", None, None),
        P("owner", "dp"),
        P(),
    )
    return jax.shard_map(local, mesh=mesh, in_specs=in_specs, out_specs=P(), check_vma=False)
```

```python
import functools
import math

import jax
import jax.numpy as jnp
from jax import lax
from jax.experimental import pallas as pl
from jax.experimental.pallas import tpu as pltpu
from jax.sharding import PartitionSpec as P

NQ = 8
ET = 16
DAMPING = 0.1
MESH = pl.DeviceIdType.MESH
F32 = jnp.float32
BF16 = jnp.bfloat16


def flipped(index, mask, bits):
    for k in range(bits):
        if mask >> k & 1:
            index = index + (1 << k) - (2 << k) * (index // (1 << k) % 2)
    return index


def kernel(
    n, m, local_q, example_count, scale,
    map_ref, query_out, train_out, query_in, train_in, basis_out_hbm, basis_in_hbm, eig_hbm,
    scores_ref,
    gathered, in_tok, cols, basis_out, basis_in, eig, masked, act, acc, parts, owner_parts,
    ag_send, ag_recv, core_send, core_recv, a2a_send, a2a_recv, load_sem,
    part_send, part_recv, own_send, own_recv,
):
    d = lax.axis_index("dp")
    o = lax.axis_index("owner")
    bits = n.bit_length() - 1
    partner = flipped(o, 1, 1)
    capacity, width = basis_out.shape[0], basis_out.shape[1]
    blocks = query_out.shape[1] // width
    units = eig.shape[1]
    in_blocks, in_width = basis_in.shape[0], basis_in.shape[1]
    per_device = local_q + train_out.shape[0]
    rows = n * per_device
    half = blocks // 2
    own = o % 2 * blocks

    loads = [
        pltpu.make_async_copy(basis_in_hbm, basis_in, load_sem.at[0]),
        pltpu.make_async_copy(basis_out_hbm, basis_out, load_sem.at[1]),
        pltpu.make_async_copy(eig_hbm, eig, load_sem.at[2]),
    ]
    for load in loads:
        load.start()
    barrier = pltpu.get_barrier_semaphore()
    for r in range(1, n):
        pl.semaphore_signal(
            barrier, inc=1, device_id={"dp": (d + r) % n, "owner": o}, device_id_type=MESH
        )
    for r in range(1, m):
        pl.semaphore_signal(
            barrier, inc=1, device_id={"dp": d, "owner": (o + r) % m}, device_id_type=MESH
        )

    def packed(query_ref, train_ref, at):
        both = (query_ref[:, at].astype(F32), train_ref[:, at].astype(F32))
        return jnp.concatenate(both, 0).astype(BF16)

    for b in range(blocks):
        gathered[d, own + b] = packed(
            query_out, train_out, slice(b * width, (b + 1) * width)
        )
    for j in range(n):
        in_tok[j] = packed(query_in, train_in, slice(j * units, (j + 1) * units))
    cols[d] = in_tok[d]
    pl.semaphore_wait(barrier, n - 1 + m - 1)

    def piece(h, mask):
        return gathered.at[flipped(d, mask, bits), pl.ds(own + h * half, half)]

    def far_piece(h, mask):
        return gathered.at[
            flipped(d, mask, bits), pl.ds(blocks - own + h * half, half)
        ]

    def gather_copy(h, mask, k):
        return pltpu.make_async_remote_copy(
            src_ref=piece(h, mask),
            dst_ref=piece(h, mask),
            send_sem=ag_send.at[h, mask ^ (1 << k)],
            recv_sem=ag_recv.at[h, mask ^ (1 << k)],
            device_id={"dp": flipped(d, 1 << k, bits), "owner": o},
            device_id_type=MESH,
        )

    def gather_arrival(h, mask):
        return pltpu.make_async_remote_copy(
            src_ref=piece(h, mask),
            dst_ref=piece(h, mask),
            send_sem=ag_send.at[h, mask],
            recv_sem=ag_recv.at[h, mask],
            device_id={"dp": flipped(d, 1, bits), "owner": o},
            device_id_type=MESH,
        )

    def core_copy(h, mask, ref):
        return pltpu.make_async_remote_copy(
            src_ref=ref,
            dst_ref=ref,
            send_sem=core_send.at[h, mask],
            recv_sem=core_recv.at[h, mask],
            device_id={"dp": d, "owner": partner},
            device_id_type=MESH,
        )

    def column_copy(r):
        return pltpu.make_async_remote_copy(
            src_ref=in_tok.at[(d + r) % n],
            dst_ref=cols.at[d],
            send_sem=a2a_send.at[r],
            recv_sem=a2a_recv.at[r],
            device_id={"dp": (d + r) % n, "owner": o},
            device_id_type=MESH,
        )

    def column_arrival(r):
        source = (d + n - r) % n
        return pltpu.make_async_remote_copy(
            src_ref=in_tok.at[source],
            dst_ref=cols.at[source],
            send_sem=a2a_send.at[r],
            recv_sem=a2a_recv.at[r],
            device_id={"dp": source, "owner": o},
            device_id_type=MESH,
        )

    first = list(range(bits - 1, -1, -1))
    second = first[:-2] + first[-2:][::-1]
    orders = (first, second)
    sent = []

    local_t = per_device - local_q
    train_rows = n * local_t
    token = lax.broadcasted_iota(jnp.int32, (train_rows, rows), 0)
    place = token // local_t * per_device + local_q + token % local_t
    at_row = lax.broadcasted_iota(jnp.int32, (train_rows, rows), 1)
    pick = jnp.where(place == at_row, 1.0, 0.0).astype(BF16)

    def prepare():
        for r in range(1, n):
            column_arrival(r).wait_recv()
        loads[0].wait()
        row = lax.broadcasted_iota(jnp.int32, (rows, in_width), 0)
        inside = row % per_device
        token = row // per_device * local_q + inside
        per_query = n * local_q // NQ
        owner_query = jnp.where(inside < local_q, token // per_query, NQ)
        for j in range(in_blocks):
            at = slice(j * in_width, (j + 1) * in_width)
            columns = cols[:, :, at].reshape(rows, in_width)
            turned = jnp.dot(columns, basis_in[j], preferred_element_type=F32)
            act[:, at] = jnp.dot(
                pick, turned.astype(BF16), preferred_element_type=F32
            ).astype(BF16)
            for q in range(NQ):
                masked[q, :, at] = jnp.where(owner_query == q, turned, 0.0).astype(BF16)

    def begin(copy):
        copy.start()
        sent.append(copy)

    def arrived_at(h, mask):
        return max(p for p in range(bits) if mask >> orders[h][p] & 1)

    def pass_on(h, mask, position):
        for k in orders[h][position:]:
            begin(gather_copy(h, mask, k))
        begin(core_copy(h, mask, piece(h, mask)))

    for h in range(2):
        pass_on(h, 0, 0)
    for r in range(1, n):
        begin(column_copy(r))
    arrivals = [(h, mask) for mask in range(1, n) for h in range(2)]
    arrivals.sort(key=lambda a: (a[1].bit_count(), arrived_at(*a)))
    for h, mask in arrivals:
        if arrived_at(h, mask) < bits - 1:
            gather_arrival(h, mask).wait_recv()
            pass_on(h, mask, arrived_at(h, mask) + 1)
    prepare()
    for h, mask in arrivals:
        if arrived_at(h, mask) == bits - 1:
            gather_arrival(h, mask).wait_recv()
            pass_on(h, mask, bits)
    for h in range(2):
        for mask in range(n):
            core_copy(h, mask, far_piece(h, mask)).wait_recv()
    for load in loads[1:]:
        load.wait()

    acc[...] = jnp.zeros_like(acc)
    base = o // 2 * 2 * blocks
    ranks, held = [], []
    count = 0
    for c in range(2 * blocks):
        mine = (map_ref[base + c] == o).astype(jnp.int32)
        held.append(mine)
        ranks.append(count)
        count = count + mine

    together = next(g for g in (4, 3, 2, 1) if capacity % g == 0)

    def some_slots(s, carry):
        lefts, rights = [], []
        for g in range(together):
            slot = s * together + g
            block = 0
            for c in range(2 * blocks):
                block = block + c * held[c] * (ranks[c] == slot).astype(jnp.int32)
            tokens = gathered[:, block].reshape(rows, width)
            turned = jnp.dot(tokens, basis_out[slot], preferred_element_type=F32)
            turned = jnp.where(slot < count, turned, 0.0)
            turned_t = turned.T
            lefts.append(turned_t.astype(BF16))
            rights.append(jnp.dot(pick, turned.astype(BF16), preferred_element_type=F32).astype(BF16))
        left = jnp.concatenate(lefts, 0)
        right = jnp.concatenate(rights, 1)
        start = pl.multiple_of(s * together * width, together * width)
        weight = 1.0 / (eig[pl.ds(start, together * width), :] + DAMPING)
        for q in range(NQ):
            moment = jnp.dot(left, masked[q], preferred_element_type=F32)
            damped = (moment * weight).astype(BF16)
            acc[q] += jnp.dot(right, damped, preferred_element_type=F32)
        return carry

    lax.fori_loop(0, capacity // together, some_slots, 0)

    per_token = jnp.sum(acc[...] * act[...].astype(F32)[None], axis=2)
    token = lax.broadcasted_iota(jnp.int32, (train_rows, 128), 0)
    example = lax.broadcasted_iota(jnp.int32, (train_rows, 128), 1)
    hot = jnp.where(token // ET == example, 1.0, 0.0)
    mine = jnp.dot(
        per_token, hot, precision=lax.Precision.HIGHEST, preferred_element_type=F32
    )

    parts[d] = mine

    def part_copy(r, source):
        return pltpu.make_async_remote_copy(
            src_ref=parts.at[source],
            dst_ref=parts.at[source],
            send_sem=part_send.at[r],
            recv_sem=part_recv.at[r],
            device_id={"dp": (d + r) % n, "owner": o},
            device_id_type=MESH,
        )

    def owner_copy(r, source):
        return pltpu.make_async_remote_copy(
            src_ref=owner_parts.at[source],
            dst_ref=owner_parts.at[source],
            send_sem=own_send.at[r],
            recv_sem=own_recv.at[r],
            device_id={"dp": d, "owner": (o + r) % m},
            device_id_type=MESH,
        )

    for r in range(1, n):
        copy = part_copy(r, d)
        copy.start()
        sent.append(copy)
    for r in range(1, n):
        part_copy(r, (d + n - r) % n).wait_recv()
    owner_parts[o] = jnp.sum(parts[...], axis=0)
    for r in range(1, m):
        copy = owner_copy(r, o)
        copy.start()
        sent.append(copy)
    for r in range(1, m):
        owner_copy(r, (o + m - r) % m).wait_recv()
    total = jnp.sum(owner_parts[...], axis=0) * scale
    scores_ref[...] = total[:, :example_count]
    for copy in sent:
        copy.wait_send()


def local(query_out, query_in, train_out, train_in, basis_out, basis_in, eigvals, owner_map):
    n = lax.axis_size("dp")
    m = lax.axis_size("owner")
    capacity, width = basis_out.shape[0], basis_out.shape[1]
    local_q = query_out.shape[0]
    per_device = local_q + train_out.shape[0]
    blocks = query_out.shape[1] // width
    units = eigvals.shape[1]
    rows = n * per_device
    example_count = n * train_out.shape[0] // ET
    hidden_total = query_out.shape[1] * m
    per_query = n * local_q // NQ
    scale = 1.0 / math.sqrt(per_query * ET * hidden_total * query_in.shape[1])
    vmem = pl.BlockSpec(memory_space=pltpu.VMEM)
    anywhere = pl.BlockSpec(memory_space=pl.ANY)
    dma = pltpu.SemaphoreType.DMA
    return pl.pallas_call(
        functools.partial(kernel, n, m, local_q, example_count, scale),
        out_shape=jax.ShapeDtypeStruct((NQ, example_count), F32),
        in_specs=[
            pl.BlockSpec(memory_space=pltpu.SMEM),
            vmem,
            vmem,
            vmem,
            vmem,
            anywhere,
            anywhere,
            anywhere,
        ],
        out_specs=vmem,
        scratch_shapes=[
            pltpu.VMEM((n, 2 * blocks, per_device, width), BF16),
            pltpu.VMEM((n, per_device, units), BF16),
            pltpu.VMEM((n, per_device, units), BF16),
            pltpu.VMEM(basis_out.shape, BF16),
            pltpu.VMEM(basis_in.shape, BF16),
            pltpu.VMEM(eigvals.shape, F32),
            pltpu.VMEM((NQ, rows, units), BF16),
            pltpu.VMEM((n * train_out.shape[0], units), BF16),
            pltpu.VMEM((NQ, n * train_out.shape[0], units), F32),
            pltpu.VMEM((n, NQ, 128), F32),
            pltpu.VMEM((m, NQ, 128), F32),
            dma((2, n)),
            dma((2, n)),
            dma((2, n)),
            dma((2, n)),
            dma((n,)),
            dma((n,)),
            dma((3,)),
            dma((n,)),
            dma((n,)),
            dma((m,)),
            dma((m,)),
        ],
        compiler_params=pltpu.CompilerParams(
            collective_id=0, has_side_effects=True, vmem_limit_bytes=56 * 2**20
        ),
    )(owner_map, query_out, train_out, query_in, train_in, basis_out, basis_in, eigvals)


def solution(mesh):
    in_specs = (
        P("dp", "owner"),
        P("dp", None),
        P("dp", "owner"),
        P("dp", None),
        P("owner", None, None),
        P("dp", None, None),
        P("owner", "dp"),
        P(),
    )
    return jax.shard_map(local, mesh=mesh, in_specs=in_specs, out_specs=P(), check_vma=False)
```
